256 devices in a mesh: occ: 16 (over x, y), vr: 8 (over z), vc: 2 (over core).
Axes of the slice: x: 4, y: 4, z: 8, core: 2. Of those that a mesh axis runs over, the one named last changes fastest.
Arguments:
- ladder_amps: float32 [1024, 12288], P('occ', ('vr', 'vc')), may hold values from -6 to 6
- vvvv_slice: float32 [12288, 47104], P('occ', ('vr', 'vc')), may hold values from -0.0546875 to 0.0546875
- cd_live: int32 [192], P('occ'), may hold values 0 or 1
- amplitudes: float32 [1024, 47104], P('occ', ('vr', 'vc')), may hold values from -6 to 6
- hole_inter: float32 [1024, 1024], P('occ', ('vr', 'vc')), may hold values from -0.1875 to 0.1875
- direct: float32 [1024, 47104], P('occ', ('vr', 'vc')), may hold values from -6 to 6
- occ_energy: float32 [1024], P('occ'), may hold values from -3 to -1
- vir_energy: float32 [47104], P(('vr', 'vc')), may hold values from 1 to 4
Outputs:
- new_amps: float32 [1024, 47104], P('occ', ('vr', 'vc'))
The draws below stay inside these ranges and needn't reach their ends.
All inputs are finite; a program needn't handle non-finite values. No bound on the sum of `cd_live` on one device may be relied on, other than what follows from the above.
Results may differ from the reference program's by a relative error of at most 0.000057.
Values sent between devices are 32-bit elements; how exact they have to be, the bound alone decides.
No kernel may reach another device: no remote copies, remote signals or barrier semaphores. Data moves between devices by JAX's collectives and lax.ppermute only.
A program may use at most 128 MiB of HBM per device.

```python
import jax
import jax.numpy as jnp
from jax import lax

BLOCK = 64
IJ = 1024
CD = 12288
AB = 47104


def touch_ends(array, key, low, largest):
    dims = array.shape
    place = [jax.random.randint(jax.random.fold_in(key, axis), (), 0, dims[axis]) for axis in range(len(dims))]
    array = array.at[tuple(place)].set(low)
    longest = dims.index(max(dims))
    place[longest] = (place[longest] + 1) % dims[longest]
    return array.at[tuple(place)].set(largest)


def shard_levels(stream_key, extent, split, smallest, largest):
    level = 1.0
    for dim, blocks in split:
        heights = jax.random.uniform(jax.random.fold_in(jax.random.fold_in(stream_key, 6), dim), (blocks,), jnp.float32, smallest / len(split), largest / len(split))
        level = level * jnp.repeat(jnp.exp(heights), extent[dim] // blocks).reshape((-1,) + (1,) * (len(extent) - 1 - dim))
    return level


def gaussian(rng, dims, width, reach, split=(), held_as=jnp.bfloat16):
    gain = shard_levels(rng, dims, split, -0.22, 0.18) if split else 1.0
    array = jax.random.normal(rng, dims, jnp.float32) * width * gain
    return jnp.minimum(jnp.maximum(array, -reach), reach).astype(held_as)


def setup_inputs(seed: int = 0) -> dict:
    streams_of = jax.random.split(jax.random.key(seed), 9)
    return {
        "ladder_amps": gaussian(streams_of[0], (IJ, CD), 1.0, 6.0, ((0, 16), (1, 16)), jnp.float32),
        "vvvv_slice": gaussian(streams_of[1], (CD, AB), CD ** -0.5, 0.0546875, ((0, 16), (1, 16)), jnp.float32),
        "cd_live": touch_ends((jax.random.randint(streams_of[2], (CD // BLOCK,), 0, 4) < 3).astype(jnp.int32), jax.random.fold_in(streams_of[2], 1), 0, 1),
        "amplitudes": gaussian(streams_of[3], (IJ, AB), 1.0, 6.0, ((0, 16), (1, 16)), jnp.float32),
        "hole_inter": gaussian(streams_of[4], (IJ, IJ), IJ ** -0.5, 0.1875, ((0, 16), (1, 16)), jnp.float32),
        "direct": gaussian(streams_of[5], (IJ, AB), 1.0, 6.0, ((0, 16), (1, 16)), jnp.float32),
        "occ_energy": jnp.clip(-3.0 + 2.0 * jax.random.uniform(streams_of[6], (IJ,), jnp.float32) ** shard_levels(streams_of[6], (IJ,), ((0, 16),), -0.2, 0.2), -3.0, -1.0),
        "vir_energy": jnp.clip(1.0 + 3.0 * jax.random.uniform(streams_of[7], (AB,), jnp.float32) ** shard_levels(streams_of[7], (AB,), ((0, 16),), -0.2, 0.2), 1.0, 4.0),
    }


def reference(ladder_amps, vvvv_slice, cd_live, amplitudes, hole_inter, direct, occ_energy, vir_energy):
    highest = lax.Precision.HIGHEST
    live_cols = jnp.repeat(cd_live.astype(jnp.float32), BLOCK)
    masked = ladder_amps * live_cols[None, :]
    ladder = jnp.dot(masked, vvvv_slice, precision=highest, preferred_element_type=jnp.float32)
    hole_term = jnp.dot(hole_inter, amplitudes, precision=highest, preferred_element_type=jnp.float32)
    residue = direct + ladder + hole_term
    return residue / (vir_energy[None, :] - occ_energy[:, None])
```

```python
import jax
import jax.numpy as jnp
from jax import lax
from jax.sharding import PartitionSpec as P

BLOCK = 64


def on_device(
    ladder_amps, vvvv_slice, cd_live, amplitudes, hole_inter, direct, occ_energy, vir_energy
):
    n = lax.axis_size("occ")
    swap = [(o * n + c, c * n + o) for o in range(n) for c in range(n)]
    mine = jnp.concatenate([ladder_amps, hole_inter], axis=1)
    mine = lax.ppermute(mine, ("occ", "vr", "vc"), swap)
    live_cols = jnp.repeat(cd_live.astype(jnp.float32), BLOCK)
    keep = jnp.concatenate([live_cols, jnp.ones((hole_inter.shape[1],), jnp.float32)])
    left = lax.all_gather(mine * keep[None, :], ("vr", "vc"), axis=0, tiled=True)
    right = jnp.concatenate([vvvv_slice, amplitudes], axis=0)
    terms = jnp.dot(left, right, precision=lax.Precision.HIGH, preferred_element_type=jnp.float32)
    summed = lax.psum_scatter(terms, "occ", scatter_dimension=0, tiled=True)
    return (direct + summed) / (vir_energy[None, :] - occ_energy[:, None])


def solution(mesh):
    in_specs = (
        P("occ", ("vr", "vc")),
        P("occ", ("vr", "vc")),
        P("occ"),
        P("occ", ("vr", "vc")),
        P("occ", ("vr", "vc")),
        P("occ", ("vr", "vc")),
        P("occ"),
        P(("vr", "vc")),
    )
    out_specs = P("occ", ("vr", "vc"))
    return jax.shard_map(
        on_device, mesh=mesh, in_specs=in_specs, out_specs=out_specs, check_vma=False
    )
```

```python
import functools

import jax
import jax.numpy as jnp
import numpy as np
from jax import lax
from jax.experimental import pallas as pl
from jax.experimental.pallas import tpu as pltpu
from jax.sharding import PartitionSpec as P

BLOCK = 64
AXES = ("occ", "vr", "vc")
NX, NY, NZ, NC = 4, 4, 8, 2
TILE = 512
COST = 1000
SIZES = (64,)
ROUNDS = ((0, 3), (3, 6))
ORDER = (
    (2, 0), (2, 1), (1, 2), (1, 3),
    (2, 2), (2, 3), (3, 0), (3, 1),
    (1, 0), (1, 1),
    (3, 2), (3, 3),
    (0, 0), (0, 1), (0, 2), (0, 3),
)
PARTS = (4, 4, 2, 2, 4)


def place(x, y, z, k):
    return (((x % NX) * NY + y % NY) * NZ + z % NZ) * NC + k % NC


def pairs(fn):
    out = []
    for x in range(NX):
        for y in range(NY):
            for z in range(NZ):
                for k in range(NC):
                    out.append((place(x, y, z, k), place(*fn(x, y, z, k))))
    return out


def first(d):
    return pairs(lambda x, y, z, k: (x + d, y, z, k) if k == 0 else (x, y + d, z, k))


def second(d):
    return pairs(lambda x, y, z, k: (x, y + d, z, k) if k == 0 else (x + d, y, z, k))


FROM = (6, 3, 4, 7, 4, 1, 0, 6, 0, 4, 6, 2, 3, 7, 1, 5)
TO = (3, 1, 0, 2, 2, 4, 7, 6, 1, 6, 0, 5, 7, 5, 3, 4)
CORE = (1, 1, 0, 1, 0, 1, 0, 0, 0, 1, 1, 1, 1, 0, 0, 0)


def to_slots(x, y, z, k):
    c, o = z * NC + k, x * NY + y
    return c // NY, c % NY, FROM[c] + TO[o], CORE[o]


def places():
    table = np.zeros((NX * NY * NZ * NC, len(ORDER)), np.int32)
    for x in range(NX):
        for y in range(NY):
            for z in range(NZ):
                for k in range(NC):
                    for q, (a, b) in enumerate(ORDER):
                        o = (x + a) % NX * NY + (y + b) % NY if k == 0 else (x + b) % NX * NY + (y + a) % NY
                        home = FROM[x * NY + y] + TO[o]
                        steps = (z - home if k == 0 else home - z) % NZ
                        other = int(CORE[o] != k)
                        if steps < 4:
                            at = 2 * steps + other
                        elif steps == 4:
                            at = 15 if other else 8
                        else:
                            at = 9 + 2 * (NZ - 1 - steps) + 1 - other
                        table[place(x, y, z, k), q] = at
    return table


SLOTS = pairs(to_slots)
ALONG_Z = pairs(lambda x, y, z, k: (x, y, z + (1 if k == 0 else -1), k))
OTHER = pairs(lambda x, y, z, k: (x, y, z, 1 - k))


def send(x, p):
    return lax.ppermute(x, AXES, p)


def split(x):
    hi = x.astype(jnp.bfloat16)
    return hi, (x - hi.astype(jnp.float32)).astype(jnp.bfloat16)


def prepare_kernel(v_ref, a_ref, hi_ref, lo_ref, tail_ref):
    hi, lo = split(v_ref[...])
    hi_ref[...] = hi
    lo_ref[...] = lo
    ah, al = split(a_ref[...])
    tail_ref[...] = jnp.concatenate([ah, al, ah], axis=0)


def prepare(v, a):
    v = pltpu.with_memory_space_constraint(v, pltpu.HBM)
    cd, n = v.shape
    o = a.shape[0]
    col = lambda i: (0, i)
    return pl.pallas_call(
        prepare_kernel,
        grid=(pl.cdiv(n, TILE),),
        in_specs=[pl.BlockSpec((cd, TILE), col), pl.BlockSpec((o, TILE), col)],
        out_specs=[pl.BlockSpec((cd, TILE), col), pl.BlockSpec((cd, TILE), col), pl.BlockSpec((3 * o, TILE), col)],
        out_shape=[
            pltpu.HBM((cd, n), jnp.bfloat16),
            pltpu.HBM((cd, n), jnp.bfloat16),
            pltpu.HBM((3 * o, n), jnp.bfloat16),
        ],
        compiler_params=pltpu.CompilerParams(vmem_limit_bytes=32 << 20),
        cost_estimate=pl.CostEstimate(flops=4 * cd * n, bytes_accessed=8 * (cd + o) * n, transcendentals=0),
        name="prepare",
    )(v, a)


def product_kernel(n_src, cd, parts, idx_ref, *refs):
    x_refs, (keep_ref, hi_ref, lo_ref, tail_ref) = refs[:n_src], refs[n_src : n_src + 4]
    outs, (x_all, lh, ll, lt) = refs[n_src + 4 : n_src + 4 + len(parts)], refs[n_src + 4 + len(parts) :]
    r = x_all.shape[1]

    @pl.when(pl.program_id(0) == 0)
    def _():
        at = 0
        for x_ref in x_refs:
            x_all[at : at + x_ref.shape[0]] = x_ref[...]
            at += x_ref.shape[0]
        for q in range(sum(parts)):
            hi, lo = split(x_all[idx_ref[q]] * keep_ref[...])
            rows = slice(q * r, (q + 1) * r)
            lh[rows, :] = hi[:, :cd]
            ll[rows, :] = lo[:, :cd]
            lt[rows, :] = jnp.concatenate([hi[:, cd:], hi[:, cd:], lo[:, cd:]], axis=1)

    dot = functools.partial(jnp.dot, preferred_element_type=jnp.float32)
    out = (
        dot(lh[...], hi_ref[...])
        + dot(lh[...], lo_ref[...])
        + dot(ll[...], hi_ref[...])
        + dot(lt[...], tail_ref[...])
    )
    at = 0
    for part, o_ref in zip(parts, outs):
        o_ref[...] = out[at * r : (at + part) * r]
        at += part


def product(idx, xs, r, keep, right, parts, tiles):
    hi, lo, tail = (pltpu.with_memory_space_constraint(x, pltpu.HBM) for x in right)
    cd, n = hi.shape
    k = keep.shape[1]
    xs = [x.reshape(-1, r, k) for x in xs]
    m = sum(parts) * r
    lo_tile, hi_tile = tiles
    width = min(hi_tile * TILE, n) - lo_tile * TILE
    col = lambda i, *_: (0, lo_tile + i)
    return pl.pallas_call(
        functools.partial(product_kernel, len(xs), cd, parts),
        grid_spec=pltpu.PrefetchScalarGridSpec(
            num_scalar_prefetch=1,
            grid=(hi_tile - lo_tile,),
            in_specs=[pl.BlockSpec(x.shape, lambda i, *_: (0, 0, 0)) for x in xs]
            + [
                pl.BlockSpec(keep.shape, lambda i, *_: (0, 0)),
                pl.BlockSpec((cd, TILE), col),
                pl.BlockSpec((cd, TILE), col),
                pl.BlockSpec((tail.shape[0], TILE), col),
            ],
            out_specs=[pl.BlockSpec((p * r, TILE), lambda i, *_: (0, i)) for p in parts],
            scratch_shapes=[
                pltpu.VMEM((NZ * NC, r, k), jnp.float32),
                pltpu.VMEM((m, cd), jnp.bfloat16),
                pltpu.VMEM((m, cd), jnp.bfloat16),
                pltpu.VMEM((m, tail.shape[0]), jnp.bfloat16),
            ],
        ),
        out_shape=[jax.ShapeDtypeStruct((p * r, width), jnp.float32) for p in parts],
        compiler_params=pltpu.CompilerParams(vmem_limit_bytes=32 << 20),
        cost_estimate=pl.CostEstimate(flops=COST, bytes_accessed=COST, transcendentals=0),
        name="product",
    )(idx, *xs, keep, hi, lo, tail)


def after(x, *deps):
    return lax.optimization_barrier((x, *deps))[0]


def ring_z(pair, right):
    r = pair.shape[0] // 2
    chain, back = [pair], []
    for step in range(3):
        chain.append(send(after(chain[-1], *right) if step == 1 else chain[-1], ALONG_Z))
        back.append(send(chain[-1], OTHER))
    far = send(chain[3][:r], ALONG_Z)
    return chain + [far] + back + [send(far, OTHER)]


def on_device(
    ladder_amps, vvvv_slice, cd_live, amplitudes, hole_inter, direct, occ_energy, vir_energy
):
    z, core = lax.axis_index("vr"), lax.axis_index("vc")
    mine = jnp.concatenate([ladder_amps, hole_inter], axis=1)
    live_cols = jnp.repeat(cd_live.astype(jnp.float32), BLOCK)
    keep = jnp.concatenate([live_cols, jnp.ones((hole_inter.shape[1],), jnp.float32)])[None, :]

    device = (lax.axis_index("occ") * NZ + z) * NC + core
    idx = lax.dynamic_slice_in_dim(jnp.asarray(places()), device, 1, 0)[0]
    n_first = sum(PARTS[:2])

    mine = send(mine, SLOTS)
    other = send(mine, OTHER)
    right = prepare(after(vvvv_slice, other), amplitudes)
    rounds, at = [], 0
    for r in SIZES:
        xs = ring_z(jnp.concatenate([mine[at : at + r], other[at : at + r]]), right)
        rounds += [(r, tiles, xs) for tiles in ROUNDS]
        at += r

    firsts, deps = [], ()
    for r, tiles, xs in rounds:
        s1p, s1m = product(after(idx[:n_first], *deps), xs, r, keep, right, PARTS[:2], tiles)
        firsts.append((send(s1p, first(1)), send(s1m, first(-1))))
        deps = (send(s1m[:8, :128], OTHER),)

    seconds = []
    for (r, tiles, xs), (r1p, r1m) in zip(rounds, firsts):
        mp, mm, own = deps = product(after(idx[n_first:], *deps), xs, r, keep, right, PARTS[2:], tiles)
        r2p, r2m = send(mp + r1p[: 2 * r], first(1)), send(mm + r1m[: 2 * r], first(-1))
        seconds.append((own[: 2 * r] + r2p + r1m[2 * r :], own[2 * r :] + r1p[2 * r :] + r2m))

    summed = []
    for (r, _, _), (g01, g23) in zip(rounds, seconds):
        h = r // 2
        t1p = jnp.concatenate([g23[:h], g01[r + h :]])
        t1m = jnp.concatenate([g23[h:r], g23[r : r + h]])
        u1p, u1m = send(t1p, second(1)), send(t1m, second(-1))
        u2p, u2m = send(g01[r : r + h] + u1p[:h], second(1)), send(g23[r + h :] + u1m[:h], second(-1))
        summed.append(jnp.concatenate([g01[:h] + u2p + u1m[h:], g01[h:r] + u1p[h:] + u2m]))
    n = len(ROUNDS)
    summed = [jnp.concatenate(summed[i : i + n], axis=1) for i in range(0, len(summed), n)]
    summed = jnp.concatenate(summed)
    return (direct + summed) / (vir_energy[None, :] - occ_energy[:, None])


def solution(mesh):
    in_specs = (
        P("occ", ("vr", "vc")),
        P("occ", ("vr", "vc")),
        P("occ"),
        P("occ", ("vr", "vc")),
        P("occ", ("vr", "vc")),
        P("occ", ("vr", "vc")),
        P("occ"),
        P(("vr", "vc")),
    )
    out_specs = P("occ", ("vr", "vc"))
    return jax.shard_map(
        on_device, mesh=mesh, in_specs=in_specs, out_specs=out_specs, check_vma=False
    )
```

```python
import functools

import jax
import jax.numpy as jnp
import numpy as np
from jax import lax
from jax.experimental import pallas as pl
from jax.experimental.pallas import tpu as pltpu
from jax.sharding import PartitionSpec as P

BLOCK = 64
AXES = ("occ", "vr", "vc")
NX, NY, NZ, NC = 4, 4, 8, 2
TILE = 512
COST = 1000
STREAMS = 2
ROUNDS = ((0, 3), (3, 6))
ORDER = (
    (2, 0), (2, 1), (1, 2), (1, 3),
    (2, 2), (2, 3), (3, 0), (3, 1),
    (1, 0), (1, 1),
    (3, 2), (3, 3),
    (0, 0), (0, 1), (0, 2), (0, 3),
)
PARTS = (4, 4, 2, 2, 4)


def place(x, y, z, k):
    return (((x % NX) * NY + y % NY) * NZ + z % NZ) * NC + k % NC


def pairs(fn):
    out = []
    for x in range(NX):
        for y in range(NY):
            for z in range(NZ):
                for k in range(NC):
                    out.append((place(x, y, z, k), place(*fn(x, y, z, k))))
    return out


def first(d):
    return pairs(lambda x, y, z, k: (x + d, y, z, k) if k == 0 else (x, y + d, z, k))


def second(d):
    return pairs(lambda x, y, z, k: (x, y + d, z, k) if k == 0 else (x + d, y, z, k))


FROM = (6, 3, 4, 7, 4, 1, 0, 6, 0, 4, 6, 2, 3, 7, 1, 5)
TO = (3, 1, 0, 2, 2, 4, 7, 6, 1, 6, 0, 5, 7, 5, 3, 4)
CORE = (1, 1, 0, 1, 0, 1, 0, 0, 0, 1, 1, 1, 1, 0, 0, 0)


def to_slots(x, y, z, k):
    c, o = z * NC + k, x * NY + y
    return c // NY, c % NY, FROM[c] + TO[o], CORE[o]


def places():
    table = np.zeros((NX * NY * NZ * NC, len(ORDER)), np.int32)
    for x in range(NX):
        for y in range(NY):
            for z in range(NZ):
                for k in range(NC):
                    for q, (a, b) in enumerate(ORDER):
                        o = (x + a) % NX * NY + (y + b) % NY if k == 0 else (x + b) % NX * NY + (y + a) % NY
                        home = FROM[x * NY + y] + TO[o]
                        steps = (z - home if k == 0 else home - z) % NZ
                        other = int(CORE[o] != k)
                        if steps < 4:
                            at = 2 * steps + other
                        elif steps == 4:
                            at = 15 if other else 8
                        else:
                            at = 9 + 2 * (NZ - 1 - steps) + 1 - other
                        table[place(x, y, z, k), q] = at
    return table


SLOTS = pairs(to_slots)
ALONG_Z = pairs(lambda x, y, z, k: (x, y, z + (1 if k == 0 else -1), k))
OTHER = pairs(lambda x, y, z, k: (x, y, z, 1 - k))


def send(x, p):
    return lax.ppermute(x, AXES, p)


def split(x):
    hi = x.astype(jnp.bfloat16)
    return hi, (x - hi.astype(jnp.float32)).astype(jnp.bfloat16)


def product_kernel(n_src, n_deps, cd, parts, given, idx_ref, live_ref, *refs):
    x_refs, right_refs = refs[:n_src], refs[n_src : n_src + (3 if given else 2)]
    refs = refs[n_src + len(right_refs) + n_deps :]
    outs, refs = refs[: len(parts)], refs[len(parts) :]
    x_all, lh, ll, lt = refs[-4:]
    if given:
        hi_ref, lo_ref, tail_ref = right_refs
    else:
        hi_ref, lo_ref, tail_ref = refs[:3]
        hi_ref[...], lo_ref[...] = split(right_refs[0][...])
        ah, al = split(right_refs[1][...])
        tail_ref[...] = jnp.concatenate([ah, al, ah], axis=0)
    r = x_all.shape[2]

    @pl.when(pl.program_id(0) == 0)
    def _():
        column = lax.broadcasted_iota(jnp.int32, (1, x_all.shape[3]), 1)
        keep = jnp.ones(column.shape, jnp.float32)
        for i in range(cd // BLOCK):
            inside = (column >= i * BLOCK) & (column < (i + 1) * BLOCK)
            keep = jnp.where(inside, live_ref[i].astype(jnp.float32), keep)
        at = 0
        for i in range(0, 5 * STREAMS, STREAMS):
            here = x_refs[i].shape[0]
            for s in range(STREAMS):
                x_all[s, at : at + here] = x_refs[i + s][...]
            at += here
        for x_ref in x_refs[5 * STREAMS :]:
            here = x_ref.shape[0] // STREAMS
            for s in range(STREAMS):
                x_all[s, at : at + here] = x_ref[s * here : (s + 1) * here]
            at += here
        for q in range(sum(parts)):
            for s in range(STREAMS):
                hi, lo = split(x_all[s, idx_ref[q]] * keep)
                rows = slice((q * STREAMS + s) * r, (q * STREAMS + s + 1) * r)
                lh[rows, :] = hi[:, :cd]
                ll[rows, :] = lo[:, :cd]
                lt[rows, :] = jnp.concatenate([hi[:, cd:], hi[:, cd:], lo[:, cd:]], axis=1)

    r *= STREAMS
    dot = functools.partial(jnp.dot, preferred_element_type=jnp.float32)
    out = (
        dot(lh[...], hi_ref[...])
        + dot(lh[...], lo_ref[...])
        + dot(ll[...], hi_ref[...])
        + dot(lt[...], tail_ref[...])
    )
    at = 0
    for part, o_ref in zip(parts, outs):
        o_ref[...] = out[at * r : (at + part) * r]
        at += part


def product(idx, live, xs, r, right, parts, tiles=None, deps=()):
    k = xs[0].shape[1]
    xs = [x.reshape(-1, r // STREAMS, k) for x in xs]
    m = sum(parts) * r
    cd = right[0].shape[0]
    o = k - cd
    col = lambda i, *_: (0, i)
    if tiles:
        right = [pltpu.with_memory_space_constraint(x, pltpu.HBM) for x in right]
        n = min(tiles[1] * TILE, right[0].shape[1]) - tiles[0] * TILE
        source = lambda i, *_: (0, tiles[0] + i)
        right_specs = [pl.BlockSpec((cd, TILE), source), pl.BlockSpec((o, TILE), source)]
        heights = (cd, cd, 3 * o)
    else:
        right = [pltpu.with_memory_space_constraint(x, pltpu.HBM) for x in right]
        n = right[0].shape[1]
        right_specs = [pl.BlockSpec((x.shape[0], TILE), col) for x in right]
        heights = ()
    out = pl.pallas_call(
        functools.partial(product_kernel, len(xs), len(deps), cd, parts, not tiles),
        grid_spec=pltpu.PrefetchScalarGridSpec(
            num_scalar_prefetch=2,
            grid=(pl.cdiv(n, TILE),),
            in_specs=[pl.BlockSpec(x.shape, lambda i, *_: (0, 0, 0)) for x in xs]
            + right_specs
            + [pl.BlockSpec(memory_space=pl.ANY)] * len(deps),
            out_specs=[pl.BlockSpec((p * r, TILE), col) for p in parts]
            + [pl.BlockSpec((h, TILE), col) for h in heights],
            scratch_shapes=[
                pltpu.VMEM((STREAMS, NZ * NC, r // STREAMS, k), jnp.float32),
                pltpu.VMEM((m, cd), jnp.bfloat16),
                pltpu.VMEM((m, cd), jnp.bfloat16),
                pltpu.VMEM((m, 3 * o), jnp.bfloat16),
            ],
        ),
        out_shape=[jax.ShapeDtypeStruct((p * r, n), jnp.float32) for p in parts]
        + [pltpu.HBM((h, n), jnp.bfloat16) for h in heights],
        compiler_params=pltpu.CompilerParams(vmem_limit_bytes=36 << 20),
        cost_estimate=pl.CostEstimate(flops=COST, bytes_accessed=COST, transcendentals=0),
        name="product",
    )(idx, live, *xs, *right, *deps)
    return out[: len(parts)], out[len(parts) :]


def ring_z(pairs):
    r = pairs[0].shape[0] // 2
    chain, back = [pairs], []
    for _ in range(3):
        chain.append([send(p, ALONG_Z) for p in chain[-1]])
        back.append(send(jnp.concatenate(chain[-1]), OTHER))
    chain.append([send(p[:r], ALONG_Z) for p in chain[3]])
    back.append(send(jnp.concatenate(chain[-1]), OTHER))
    return chain, back


def on_device(
    ladder_amps, vvvv_slice, cd_live, amplitudes, hole_inter, direct, occ_energy, vir_energy
):
    z, core = lax.axis_index("vr"), lax.axis_index("vc")
    mine = jnp.concatenate([ladder_amps, hole_inter], axis=1)
    device = (lax.axis_index("occ") * NZ + z) * NC + core
    idx = lax.dynamic_slice_in_dim(jnp.asarray(places()), device, 1, 0)[0]
    n_first = sum(PARTS[:2])

    r = mine.shape[0]
    mine = send(mine, SLOTS)
    other = send(mine, OTHER)
    parts = [slice(s * r // STREAMS, (s + 1) * r // STREAMS) for s in range(STREAMS)]
    pairs = [jnp.concatenate([mine[p], other[p]]) for p in parts]
    chain, back = ring_z(pairs)
    xs = [x for c in chain for x in c] + back

    firsts = []
    for tiles in ROUNDS:
        (s1p, s1m), right = product(idx[:n_first], cd_live, xs, r, (vvvv_slice, amplitudes), PARTS[:2], tiles)
        firsts.append((right, send(s1p, first(1)), send(s1m, first(-1))))

    seconds, deps = [], ()
    for right, r1p, r1m in reversed(firsts):
        (mp, mm, own), _ = product(idx[n_first:], cd_live, xs, r, right, PARTS[2:], deps=deps)
        deps = (mm,)
        r2p, r2m = send(mp + r1p[: 2 * r], first(1)), send(mm + r1m[: 2 * r], first(-1))
        seconds.append((own[: 2 * r] + r2p + r1m[2 * r :], own[2 * r :] + r1p[2 * r :] + r2m))
    seconds.reverse()

    summed = []
    for g01, g23 in seconds:
        near, far, back = send(g01[r:], second(1)), send(g23[:r], second(2)), send(g23[r:], second(-1))
        summed.append(g01[:r] + near + far + back)
    summed = jnp.concatenate(summed, axis=1)
    return (direct + summed) / (vir_energy[None, :] - occ_energy[:, None])


def solution(mesh):
    in_specs = (
        P("occ", ("vr", "vc")),
        P("occ", ("vr", "vc")),
        P("occ"),
        P("occ", ("vr", "vc")),
        P("occ", ("vr", "vc")),
        P("occ", ("vr", "vc")),
        P("occ"),
        P(("vr", "vc")),
    )
    out_specs = P("occ", ("vr", "vc"))
    return jax.shard_map(
        on_device, mesh=mesh, in_specs=in_specs, out_specs=out_specs, check_vma=False
    )
```

```python
import functools

import jax
import jax.numpy as jnp
import numpy as np
from jax import lax
from jax.experimental import pallas as pl
from jax.experimental.pallas import tpu as pltpu
from jax.sharding import PartitionSpec as P

BLOCK = 64
AXES = ("occ", "vr", "vc")
NX, NY, NZ, NC = 4, 4, 8, 2
TILE = 512
COST = 1000
STREAMS = 2
ROUNDS = ((0, 3), (3, 6))
ORDER = (
    (2, 0), (2, 1), (1, 2), (1, 3),
    (2, 2), (2, 3), (3, 0), (3, 1),
    (1, 0), (1, 1),
    (3, 2), (3, 3),
    (0, 0), (0, 1), (0, 2), (0, 3),
)
PARTS = (4, 4, 2, 2, 4)


def place(x, y, z, k):
    return (((x % NX) * NY + y % NY) * NZ + z % NZ) * NC + k % NC


def pairs(fn):
    out = []
    for x in range(NX):
        for y in range(NY):
            for z in range(NZ):
                for k in range(NC):
                    out.append((place(x, y, z, k), place(*fn(x, y, z, k))))
    return out


def first(d):
    return pairs(lambda x, y, z, k: (x + d, y, z, k) if k == 0 else (x, y + d, z, k))


def second(d):
    return pairs(lambda x, y, z, k: (x, y + d, z, k) if k == 0 else (x + d, y, z, k))


FROM = (6, 3, 4, 7, 4, 1, 0, 6, 0, 4, 6, 2, 3, 7, 1, 5)
TO = (3, 1, 0, 2, 2, 4, 7, 6, 1, 6, 0, 5, 7, 5, 3, 4)
CORE = (1, 1, 0, 1, 0, 1, 0, 0, 0, 1, 1, 1, 1, 0, 0, 0)


def to_slots(x, y, z, k):
    c, o = z * NC + k, x * NY + y
    return c // NY, c % NY, FROM[c] + TO[o], CORE[o]


def places():
    table = np.zeros((NX * NY * NZ * NC, len(ORDER)), np.int32)
    for x in range(NX):
        for y in range(NY):
            for z in range(NZ):
                for k in range(NC):
                    for q, (a, b) in enumerate(ORDER):
                        o = (x + a) % NX * NY + (y + b) % NY if k == 0 else (x + b) % NX * NY + (y + a) % NY
                        home = FROM[x * NY + y] + TO[o]
                        steps = (z - home if k == 0 else home - z) % NZ
                        other = int(CORE[o] != k)
                        if steps < 4:
                            at = 2 * steps + other
                        elif steps == 4:
                            at = 15 if other else 8
                        else:
                            at = 9 + 2 * (NZ - 1 - steps) + 1 - other
                        table[place(x, y, z, k), q] = at
    return table


SLOTS = pairs(to_slots)
ALONG_Z = pairs(lambda x, y, z, k: (x, y, z + (1 if k == 0 else -1), k))
OTHER = pairs(lambda x, y, z, k: (x, y, z, 1 - k))


def send(x, p):
    return lax.ppermute(x, AXES, p)


def split(x):
    hi = x.astype(jnp.bfloat16)
    return hi, (x - hi.astype(jnp.float32)).astype(jnp.bfloat16)


def product_kernel(n_src, n_deps, cd, parts, given, idx_ref, live_ref, *refs):
    x_refs, right_refs = refs[:n_src], refs[n_src : n_src + (3 if given else 2)]
    refs = refs[n_src + len(right_refs) + n_deps :]
    outs, refs = refs[: len(parts)], refs[len(parts) :]
    x_all, lh, ll, lt = refs[-4:]
    if given:
        hi_ref, lo_ref, tail_ref = right_refs
    else:
        hi_ref, lo_ref, tail_ref = refs[:3]
        hi_ref[...], lo_ref[...] = split(right_refs[0][...])
        ah, al = split(right_refs[1][...])
        tail_ref[...] = jnp.concatenate([ah, al, ah], axis=0)
    r = x_all.shape[2]

    @pl.when(pl.program_id(0) == 0)
    def _():
        column = lax.broadcasted_iota(jnp.int32, (1, x_all.shape[3]), 1)
        keep = jnp.ones(column.shape, jnp.float32)
        for i in range(cd // BLOCK):
            inside = (column >= i * BLOCK) & (column < (i + 1) * BLOCK)
            keep = jnp.where(inside, live_ref[i].astype(jnp.float32), keep)
        at = 0
        for i in range(0, 5 * STREAMS, STREAMS):
            here = x_refs[i].shape[0]
            for s in range(STREAMS):
                x_all[s, at : at + here] = x_refs[i + s][...]
            at += here
        for x_ref in x_refs[5 * STREAMS :]:
            here = x_ref.shape[0] // STREAMS
            for s in range(STREAMS):
                x_all[s, at : at + here] = x_ref[s * here : (s + 1) * here]
            at += here
        for q in range(sum(parts)):
            for s in range(STREAMS):
                hi, lo = split(x_all[s, idx_ref[q]] * keep)
                rows = slice((q * STREAMS + s) * r, (q * STREAMS + s + 1) * r)
                lh[rows, :] = hi[:, :cd]
                ll[rows, :] = lo[:, :cd]
                lt[rows, :] = jnp.concatenate([hi[:, cd:], hi[:, cd:], lo[:, cd:]], axis=1)

    r *= STREAMS
    dot = functools.partial(jnp.dot, preferred_element_type=jnp.float32)
    out = (
        dot(lh[...], hi_ref[...])
        + dot(lh[...], lo_ref[...])
        + dot(ll[...], hi_ref[...])
        + dot(lt[...], tail_ref[...])
    )
    at = 0
    for part, o_ref in zip(parts, outs):
        o_ref[...] = out[at * r : (at + part) * r]
        at += part


def product(idx, live, xs, r, right, parts, tiles=None, deps=()):
    k = xs[0].shape[1]
    xs = [x.reshape(-1, r // STREAMS, k) for x in xs]
    m = sum(parts) * r
    cd = right[0].shape[0]
    o = k - cd
    col = lambda i, *_: (0, i)
    if tiles:
        right = [pltpu.with_memory_space_constraint(x, pltpu.HBM) for x in right]
        n = min(tiles[1] * TILE, right[0].shape[1]) - tiles[0] * TILE
        source = lambda i, *_: (0, tiles[0] + i)
        right_specs = [pl.BlockSpec((cd, TILE), source), pl.BlockSpec((o, TILE), source)]
        heights = (cd, cd, 3 * o)
    else:
        right = [pltpu.with_memory_space_constraint(x, pltpu.HBM) for x in right]
        n = right[0].shape[1]
        right_specs = [pl.BlockSpec((x.shape[0], TILE), col) for x in right]
        heights = ()
    out = pl.pallas_call(
        functools.partial(product_kernel, len(xs), len(deps), cd, parts, not tiles),
        grid_spec=pltpu.PrefetchScalarGridSpec(
            num_scalar_prefetch=2,
            grid=(pl.cdiv(n, TILE),),
            in_specs=[pl.BlockSpec(x.shape, lambda i, *_: (0, 0, 0)) for x in xs]
            + right_specs
            + [pl.BlockSpec(memory_space=pl.ANY)] * len(deps),
            out_specs=[pl.BlockSpec((p * r, TILE), col) for p in parts]
            + [pl.BlockSpec((h, TILE), col) for h in heights],
            scratch_shapes=[
                pltpu.VMEM((STREAMS, NZ * NC, r // STREAMS, k), jnp.float32),
                pltpu.VMEM((m, cd), jnp.bfloat16),
                pltpu.VMEM((m, cd), jnp.bfloat16),
                pltpu.VMEM((m, 3 * o), jnp.bfloat16),
            ],
        ),
        out_shape=[jax.ShapeDtypeStruct((p * r, n), jnp.float32) for p in parts]
        + [pltpu.HBM((h, n), jnp.bfloat16) for h in heights],
        compiler_params=pltpu.CompilerParams(vmem_limit_bytes=36 << 20),
        cost_estimate=pl.CostEstimate(flops=COST, bytes_accessed=COST, transcendentals=0),
        name="product",
    )(idx, live, *xs, *right, *deps)
    return out[: len(parts)], out[len(parts) :]


def ring_z(pairs):
    r = pairs[0].shape[0] // 2
    chain, back = [pairs], []
    for _ in range(3):
        chain.append([send(p, ALONG_Z) for p in chain[-1]])
        back.append(send(jnp.concatenate(chain[-1]), OTHER))
    chain.append([send(p[:r], ALONG_Z) for p in chain[3]])
    back.append(send(jnp.concatenate(chain[-1]), OTHER))
    return chain, back


def on_device(
    ladder_amps, vvvv_slice, cd_live, amplitudes, hole_inter, direct, occ_energy, vir_energy
):
    z, core = lax.axis_index("vr"), lax.axis_index("vc")
    mine = jnp.concatenate([ladder_amps, hole_inter], axis=1)
    device = (lax.axis_index("occ") * NZ + z) * NC + core
    idx = lax.dynamic_slice_in_dim(jnp.asarray(places()), device, 1, 0)[0]
    n_first = sum(PARTS[:2])

    r = mine.shape[0]
    mine = send(mine, SLOTS)
    other = send(mine, OTHER)
    parts = [slice(s * r // STREAMS, (s + 1) * r // STREAMS) for s in range(STREAMS)]
    pairs = [jnp.concatenate([mine[p], other[p]]) for p in parts]
    chain, back = ring_z(pairs)
    xs = [x for c in chain for x in c] + back

    firsts = []
    for tiles in ROUNDS:
        (s1p, s1m), right = product(idx[:n_first], cd_live, xs, r, (vvvv_slice, amplitudes), PARTS[:2], tiles)
        firsts.append((right, send(s1p, first(1)), send(s1m, first(-1))))

    seconds, deps = [], ()
    for right, r1p, r1m in reversed(firsts):
        (mp, mm, own), _ = product(idx[n_first:], cd_live, xs, r, right, PARTS[2:], deps=deps)
        deps = (mm,)
        r2p, r2m = send(mp + r1p[: 2 * r], first(1)), send(mm + r1m[: 2 * r], first(-1))
        seconds.append((own[: 2 * r] + r2p + r1m[2 * r :], own[2 * r :] + r1p[2 * r :] + r2m))
    seconds.reverse()

    g01, g23 = (jnp.concatenate(g, axis=1) for g in zip(*seconds))
    near, far, back = send(g01[r:], second(1)), send(g23[:r], second(2)), send(g23[r:], second(-1))
    summed = g01[:r] + near + far + back
    return (direct + summed) / (vir_energy[None, :] - occ_energy[:, None])


def solution(mesh):
    in_specs = (
        P("occ", ("vr", "vc")),
        P("occ", ("vr", "vc")),
        P("occ"),
        P("occ", ("vr", "vc")),
        P("occ", ("vr", "vc")),
        P("occ", ("vr", "vc")),
        P("occ"),
        P(("vr", "vc")),
    )
    out_specs = P("occ", ("vr", "vc"))
    return jax.shard_map(
        on_device, mesh=mesh, in_specs=in_specs, out_specs=out_specs, check_vma=False
    )
```

```python
import functools

import jax
import jax.numpy as jnp
import numpy as np
from jax import lax
from jax.experimental import pallas as pl
from jax.experimental.pallas import tpu as pltpu
from jax.sharding import PartitionSpec as P

BLOCK = 64
AXES = ("occ", "vr", "vc")
NX, NY, NZ, NC = 4, 4, 8, 2
TILE = 512
COST = 1000
STREAMS = 2
ROUNDS = ((0, 2), (2, 4), (4, 6))
ORDER = (
    (2, 0), (2, 1), (1, 2), (1, 3),
    (2, 2), (2, 3), (3, 0), (3, 1),
    (1, 0), (1, 1),
    (3, 2), (3, 3),
    (0, 0), (0, 1), (0, 2), (0, 3),
)
PARTS = (4, 4, 2, 2, 4)


def place(x, y, z, k):
    return (((x % NX) * NY + y % NY) * NZ + z % NZ) * NC + k % NC


def pairs(fn):
    out = []
    for x in range(NX):
        for y in range(NY):
            for z in range(NZ):
                for k in range(NC):
                    out.append((place(x, y, z, k), place(*fn(x, y, z, k))))
    return out


def first(d):
    return pairs(lambda x, y, z, k: (x + d, y, z, k) if k == 0 else (x, y + d, z, k))


def second(d):
    return pairs(lambda x, y, z, k: (x, y + d, z, k) if k == 0 else (x + d, y, z, k))


FROM = (6, 3, 4, 7, 4, 1, 0, 6, 0, 4, 6, 2, 3, 7, 1, 5)
TO = (3, 1, 0, 2, 2, 4, 7, 6, 1, 6, 0, 5, 7, 5, 3, 4)
CORE = (1, 1, 0, 1, 0, 1, 0, 0, 0, 1, 1, 1, 1, 0, 0, 0)


def to_slots(x, y, z, k):
    c, o = z * NC + k, x * NY + y
    return c // NY, c % NY, FROM[c] + TO[o], CORE[o]


def places():
    table = np.zeros((NX * NY * NZ * NC, len(ORDER)), np.int32)
    for x in range(NX):
        for y in range(NY):
            for z in range(NZ):
                for k in range(NC):
                    for q, (a, b) in enumerate(ORDER):
                        o = (x + a) % NX * NY + (y + b) % NY if k == 0 else (x + b) % NX * NY + (y + a) % NY
                        home = FROM[x * NY + y] + TO[o]
                        steps = (z - home if k == 0 else home - z) % NZ
                        other = int(CORE[o] != k)
                        if steps < 4:
                            at = 2 * steps + other
                        elif steps == 4:
                            at = 15 if other else 8
                        else:
                            at = 9 + 2 * (NZ - 1 - steps) + 1 - other
                        table[place(x, y, z, k), q] = at
    return table


SLOTS = pairs(to_slots)
ALONG_Z = pairs(lambda x, y, z, k: (x, y, z + (1 if k == 0 else -1), k))
OTHER = pairs(lambda x, y, z, k: (x, y, z, 1 - k))


def send(x, p):
    return lax.ppermute(x, AXES, p)


def split(x):
    hi = x.astype(jnp.bfloat16)
    return hi, (x - hi.astype(jnp.float32)).astype(jnp.bfloat16)


def product_kernel(n_src, n_deps, cd, parts, given, idx_ref, live_ref, *refs):
    x_refs, right_refs = refs[:n_src], refs[n_src : n_src + (3 if given else 2)]
    refs = refs[n_src + len(right_refs) + n_deps :]
    outs, refs = refs[: len(parts)], refs[len(parts) :]
    x_all, lh, ll, lt = refs[-4:]
    if given:
        hi_ref, lo_ref, tail_ref = right_refs
    else:
        hi_ref, lo_ref, tail_ref = refs[:3]
        hi_ref[...], lo_ref[...] = split(right_refs[0][...])
        ah, al = split(right_refs[1][...])
        tail_ref[...] = jnp.concatenate([ah, al, ah], axis=0)
    r = x_all.shape[2]

    @pl.when(pl.program_id(0) == 0)
    def _():
        column = lax.broadcasted_iota(jnp.int32, (1, x_all.shape[3]), 1)
        keep = jnp.ones(column.shape, jnp.float32)
        for i in range(cd // BLOCK):
            inside = (column >= i * BLOCK) & (column < (i + 1) * BLOCK)
            keep = jnp.where(inside, live_ref[i].astype(jnp.float32), keep)
        at = 0
        for i in range(0, 5 * STREAMS, STREAMS):
            here = x_refs[i].shape[0]
            for s in range(STREAMS):
                x_all[s, at : at + here] = x_refs[i + s][...]
            at += here
        for x_ref in x_refs[5 * STREAMS :]:
            here = x_ref.shape[0] // STREAMS
            for s in range(STREAMS):
                x_all[s, at : at + here] = x_ref[s * here : (s + 1) * here]
            at += here
        for q in range(sum(parts)):
            for s in range(STREAMS):
                hi, lo = split(x_all[s, idx_ref[q]] * keep)
                rows = slice((q * STREAMS + s) * r, (q * STREAMS + s + 1) * r)
                lh[rows, :] = hi[:, :cd]
                ll[rows, :] = lo[:, :cd]
                lt[rows, :] = jnp.concatenate([hi[:, cd:], hi[:, cd:], lo[:, cd:]], axis=1)

    r *= STREAMS
    dot = functools.partial(jnp.dot, preferred_element_type=jnp.float32)
    out = (
        dot(lh[...], hi_ref[...])
        + dot(lh[...], lo_ref[...])
        + dot(ll[...], hi_ref[...])
        + dot(lt[...], tail_ref[...])
    )
    at = 0
    for part, o_ref in zip(parts, outs):
        o_ref[...] = out[at * r : (at + part) * r]
        at += part


def product(idx, live, xs, r, right, parts, tiles=None, deps=()):
    k = xs[0].shape[1]
    xs = [x.reshape(-1, r // STREAMS, k) for x in xs]
    m = sum(parts) * r
    cd = right[0].shape[0]
    o = k - cd
    col = lambda i, *_: (0, i)
    if tiles:
        right = [pltpu.with_memory_space_constraint(x, pltpu.HBM) for x in right]
        n = min(tiles[1] * TILE, right[0].shape[1]) - tiles[0] * TILE
        source = lambda i, *_: (0, tiles[0] + i)
        right_specs = [pl.BlockSpec((cd, TILE), source), pl.BlockSpec((o, TILE), source)]
        heights = (cd, cd, 3 * o)
    else:
        right = [pltpu.with_memory_space_constraint(x, pltpu.HBM) for x in right]
        n = right[0].shape[1]
        right_specs = [pl.BlockSpec((x.shape[0], TILE), col) for x in right]
        heights = ()
    out = pl.pallas_call(
        functools.partial(product_kernel, len(xs), len(deps), cd, parts, not tiles),
        grid_spec=pltpu.PrefetchScalarGridSpec(
            num_scalar_prefetch=2,
            grid=(pl.cdiv(n, TILE),),
            in_specs=[pl.BlockSpec(x.shape, lambda i, *_: (0, 0, 0)) for x in xs]
            + right_specs
            + [pl.BlockSpec(memory_space=pl.ANY)] * len(deps),
            out_specs=[pl.BlockSpec((p * r, TILE), col) for p in parts]
            + [pl.BlockSpec((h, TILE), col) for h in heights],
            scratch_shapes=[
                pltpu.VMEM((STREAMS, NZ * NC, r // STREAMS, k), jnp.float32),
                pltpu.VMEM((m, cd), jnp.bfloat16),
                pltpu.VMEM((m, cd), jnp.bfloat16),
                pltpu.VMEM((m, 3 * o), jnp.bfloat16),
            ],
        ),
        out_shape=[jax.ShapeDtypeStruct((p * r, n), jnp.float32) for p in parts]
        + [pltpu.HBM((h, n), jnp.bfloat16) for h in heights],
        compiler_params=pltpu.CompilerParams(vmem_limit_bytes=36 << 20),
        cost_estimate=pl.CostEstimate(flops=COST, bytes_accessed=COST, transcendentals=0),
        name="product",
    )(idx, live, *xs, *right, *deps)
    return out[: len(parts)], out[len(parts) :]


def ring_z(pairs):
    r = pairs[0].shape[0] // 2
    chain, back = [pairs], []
    for _ in range(3):
        chain.append([send(p, ALONG_Z) for p in chain[-1]])
        back.append(send(jnp.concatenate(chain[-1]), OTHER))
    chain.append([send(p[:r], ALONG_Z) for p in chain[3]])
    back.append(send(jnp.concatenate(chain[-1]), OTHER))
    return chain, back


def on_device(
    ladder_amps, vvvv_slice, cd_live, amplitudes, hole_inter, direct, occ_energy, vir_energy
):
    z, core = lax.axis_index("vr"), lax.axis_index("vc")
    mine = jnp.concatenate([ladder_amps, hole_inter], axis=1)
    device = (lax.axis_index("occ") * NZ + z) * NC + core
    idx = lax.dynamic_slice_in_dim(jnp.asarray(places()), device, 1, 0)[0]
    n_first = sum(PARTS[:2])

    r = mine.shape[0]
    mine = send(mine, SLOTS)
    other = send(mine, OTHER)
    parts = [slice(s * r // STREAMS, (s + 1) * r // STREAMS) for s in range(STREAMS)]
    pairs = [jnp.concatenate([mine[p], other[p]]) for p in parts]
    chain, back = ring_z(pairs)
    xs = [x for c in chain for x in c] + back

    firsts = []
    for tiles in ROUNDS:
        (s1p, s1m), right = product(idx[:n_first], cd_live, xs, r, (vvvv_slice, amplitudes), PARTS[:2], tiles)
        firsts.append((right, send(s1p, first(1)), send(s1m, first(-1))))

    seconds, deps = [], ()
    for right, r1p, r1m in reversed(firsts):
        (mp, mm, own), _ = product(idx[n_first:], cd_live, xs, r, right, PARTS[2:], deps=deps)
        deps = (mm,)
        r2p, r2m = send(mp + r1p[: 2 * r], first(1)), send(mm + r1m[: 2 * r], first(-1))
        seconds.append((own[: 2 * r] + r2p + r1m[2 * r :], own[2 * r :] + r1p[2 * r :] + r2m))
    seconds.reverse()

    g01, g23 = (jnp.concatenate(g, axis=1) for g in zip(*seconds))
    near, far, back = send(g01[r:], second(1)), send(g23[:r], second(2)), send(g23[r:], second(-1))
    summed = g01[:r] + near + far + back
    return (direct + summed) / (vir_energy[None, :] - occ_energy[:, None])


def solution(mesh):
    in_specs = (
        P("occ", ("vr", "vc")),
        P("occ", ("vr", "vc")),
        P("occ"),
        P("occ", ("vr", "vc")),
        P("occ", ("vr", "vc")),
        P("occ", ("vr", "vc")),
        P("occ"),
        P(("vr", "vc")),
    )
    out_specs = P("occ", ("vr", "vc"))
    return jax.shard_map(
        on_device, mesh=mesh, in_specs=in_specs, out_specs=out_specs, check_vma=False
    )
```
